32 devices in a mesh: dp: 4 (over y, x), mp: 8 (over z, core).
Axes of the slice: x: 2, y: 2, z: 4, core: 2. Of those that a mesh axis runs over, the one named last changes fastest.
Arguments:
- activations: bfloat16 [4096, 2048], P('dp', 'mp'), may hold values from -6 to 6
- out_grad: bfloat16 [4096, 8192], P('dp'), may hold values from -0.8984375 to 0.8984375
- old_weight: bfloat16 [8, 256, 8192], P('mp', 'dp'), may hold values from -0.125 to 0.125
- old_first: float32 [8, 256, 8192], P('mp', 'dp'), may hold values from -6 to 6
- old_second: float32 [8, 256, 8192], P('mp', 'dp'), may hold values from 0.25 to 4
- step: int32 [1], replicated, may hold values from 1 to 31
- next_input: bfloat16 [4096, 2048], P('dp', 'mp'), may hold values from -6 to 6
Outputs:
- new_weight: bfloat16 [8, 344, 8192], P('mp', 'dp')
- new_first: float32 [8, 344, 8192], P('mp', 'dp')
- new_second: float32 [8, 344, 8192], P('mp', 'dp')
- output: bfloat16 [4096, 8192], P('dp', 'mp')
The draws below stay inside these ranges and needn't reach their ends.
Inputs may be any that keep to these rules, and one draw needn't show every extreme that they name: `step`: the number of Adam steps taken, this one included.
All inputs are finite; a program needn't handle non-finite values.
Results may differ from the reference program's by a relative error of at most 0.0049.
Values may be sent and summed in bfloat16 or wider, within the bound.
A program may use at most 192 MiB of HBM per device.

```python
import math
import jax
import jax.numpy as jnp

D = 8192
HL = 256
H = 2048
NR = 86
TOKENS = 4096
N_DP = 4
N_MP = 8


def block_levels(rng, shape, pieces, smallest, high):
    def one(dim, shards_of):
        heights = jax.random.uniform(jax.random.fold_in(jax.random.fold_in(rng, 6), dim), (shards_of,), jnp.float32, smallest / len(pieces), high / len(pieces))
        return jnp.repeat(jnp.exp(heights), shape[dim] // shards_of).reshape((-1,) + (1,) * (len(shape) - dim - 1))

    gain = one(*pieces[0])
    for cut in pieces[1:]:
        gain = gain * one(*cut)
    return gain


def centred(stream_key, shape, width, most, pieces=(), kind=jnp.bfloat16):
    factor_of = block_levels(stream_key, shape, pieces, -0.22, 0.18) if pieces else 1.0
    result = jax.random.normal(stream_key, shape, jnp.float32) * width * factor_of
    return jnp.minimum(jnp.maximum(result, -most), most).astype(kind)


def setup_inputs(seed: int = 0) -> dict:
    arg_keys = jax.random.split(jax.random.key(seed), 8)
    activations = centred(arg_keys[0], (TOKENS, H), 1.0, 6.0, ((0, 4), (1, 8)))
    out_grad = centred(arg_keys[1], (TOKENS, D), 0.15, 0.8984375, ((0, 4),))
    old_weight = centred(arg_keys[2], (N_MP, HL, D), H ** -0.5, 0.125, ((0, 8), (1, 4)))
    old_first = centred(arg_keys[3], (N_MP, HL, D), 1.0, 6.0, ((0, 8), (1, 4)), jnp.float32)
    old_second = jnp.clip(jnp.exp(math.log(4.0) - 2.7725887 * jax.random.uniform(arg_keys[4], (N_MP, HL, D), jnp.float32) ** block_levels(arg_keys[4], (N_MP, HL, D), ((0, 8), (1, 4)), -0.2, 0.2)), 0.25, 4.0)
    step = jax.random.randint(arg_keys[5], (1,), 1, 32).astype(jnp.int32)
    next_input = centred(arg_keys[6], (TOKENS, H), 1.0, 6.0, ((0, 4), (1, 8)))
    return {"activations": activations, "out_grad": out_grad, "old_weight": old_weight, "old_first": old_first, "old_second": old_second, "step": step, "next_input": next_input}


def reference(activations, out_grad, old_weight, old_first, old_second, step, next_input):
    grad = jnp.dot(activations.T, out_grad, preferred_element_type=jnp.float32)
    grad = grad.reshape(N_MP, HL, D)
    extra = N_DP * NR - HL
    widths = ((0, 0), (0, extra), (0, 0))
    weight_pad = jnp.pad(old_weight, widths)
    first_pad = jnp.pad(old_first, widths)
    second_pad = jnp.pad(old_second, widths)
    grad_pad = jnp.pad(grad, widths)
    step_float = step[0].astype(jnp.float32)
    first_fix = 1.0 - jnp.power(jnp.float32(0.9), step_float)
    second_fix = 1.0 - jnp.power(jnp.float32(0.95), step_float)
    new_first = 0.9 * first_pad + 0.1 * grad_pad
    new_second = 0.95 * second_pad + 0.05 * grad_pad * grad_pad
    valid = (jnp.arange(N_DP * NR) < HL)[None, :, None]
    safe_second = jnp.where(valid, new_second, jnp.float32(1.0))
    update = new_first / first_fix / (jnp.sqrt(safe_second / second_fix) + 1e-08)
    update = jnp.where(valid, update, jnp.float32(0.0))
    new_weight = (weight_pad.astype(jnp.float32) - 0.01 * update).astype(jnp.bfloat16)
    full_weight = new_weight[:, :HL, :].reshape(H, D)
    output = jnp.dot(next_input, full_weight, preferred_element_type=jnp.float32).astype(jnp.bfloat16)
    return (new_weight, new_first, new_second, output)
```

```python
import jax
import jax.numpy as jnp
from jax import lax
from jax.sharding import PartitionSpec as P


def partner(i, k, n):
    return i ^ k if n & (n - 1) == 0 else (i + k) % n


def exchange(block, axis, k):
    n = lax.axis_size(axis)
    return lax.ppermute(block, axis, [(i, partner(i, k, n)) for i in range(n)])


def target(k, n, axis):
    me = lax.axis_index(axis)
    return me ^ k if n & (n - 1) == 0 else lax.rem(me + k, n)


def to_front(block, axis):
    n = lax.axis_size(axis)
    return lax.ppermute(block, axis, [(i, i - 1) for i in range(1, n)])


def body(activations, out_grad, old_weight, old_first, old_second, step, next_input):
    owners = lax.axis_size("dp")
    owner = lax.axis_index("dp")
    old_rows = old_weight.shape[1]
    width = old_weight.shape[2]
    held_rows = old_rows * owners
    shard_rows = (held_rows + owners - 2) // (owners - 1)
    input_all = lax.all_gather(next_input, "mp", axis=1, tiled=True)

    part = lax.dot_general(
        activations, out_grad, (((0,), (0,)), ((), ())), preferred_element_type=jnp.float32
    ).astype(jnp.bfloat16)
    part = part.reshape(owners, old_rows, width)
    grad = lax.dynamic_index_in_dim(part, owner, 0, keepdims=False).astype(jnp.float32)
    for k in range(1, owners):
        away = lax.dynamic_index_in_dim(part, target(k, owners, "dp"), 0, keepdims=False)
        grad = grad + exchange(away, "dp", k).astype(jnp.float32)

    step_float = step[0].astype(jnp.float32)
    first_fix = 1.0 - jnp.power(jnp.float32(0.9), step_float)
    second_fix = 1.0 - jnp.power(jnp.float32(0.95), step_float)
    new_first = 0.9 * old_first[0] + 0.1 * grad
    new_second = 0.95 * old_second[0] + 0.05 * grad * grad
    update = new_first / first_fix / (jnp.sqrt(new_second / second_fix) + 1e-08)
    new_weight = (old_weight[0].astype(jnp.float32) - 0.01 * update).astype(jnp.bfloat16)

    weight_part = lax.all_to_all(new_weight, "mp", split_axis=1, concat_axis=0, tiled=True)
    heads = lax.axis_size("mp")
    weight_part = weight_part.reshape(heads, old_rows, -1)
    weight_cols = lax.all_gather(weight_part, "dp", axis=1, tiled=True)
    weight_cols = weight_cols.reshape(heads * held_rows, -1)

    begin = owner * (shard_rows - old_rows)

    def mine(block):
        behind = to_front(block.astype(jnp.bfloat16), "dp").astype(block.dtype)
        rows = jnp.concatenate([block, behind, jnp.zeros((shard_rows, width), block.dtype)], 0)
        return lax.dynamic_slice_in_dim(rows, begin, shard_rows, 0)[None]

    outs = (mine(new_weight), mine(new_first), mine(new_second))
    output = jnp.dot(input_all, weight_cols, preferred_element_type=jnp.float32).astype(
        jnp.bfloat16
    )
    return (*outs, output)


def solution(mesh):
    return jax.shard_map(
        body,
        mesh=mesh,
        in_specs=(
            P("dp", "mp"),
            P("dp", None),
            P("mp", "dp", None),
            P("mp", "dp", None),
            P("mp", "dp", None),
            P(),
            P("dp", "mp"),
        ),
        out_specs=(P("mp", "dp", None), P("mp", "dp", None), P("mp", "dp", None), P("dp", "mp")),
        check_vma=False,
    )
```

```python
import functools

import jax
import jax.numpy as jnp
from jax import lax
from jax.experimental import pallas as pl
from jax.experimental.pallas import tpu as pltpu
from jax.sharding import PartitionSpec as P

MESH = pl.DeviceIdType.MESH
MIB = 1 << 20


def flip(i, k):
    for bit in (1, 2, 4, 8, 16):
        if k & bit:
            i = i + bit * (1 - 2 * ((i // bit) % 2))
    return i


def kernel(
    owners, heads,
    fix, act, og, ow, om, ov, nin,
    new_w, nxt_w, new_m, nxt_m, new_v, nxt_v, out,
    og_buf, part, own, recv, ow_buf, om_buf, ov_buf, w_buf, m_buf, v_buf, m_half, v_half,
    w_cols, in_buf, acc,
    og_sem, old_sem, new_sem, rs_send, rs_recv, a2a_send, a2a_recv, ag_send, ag_recv,
    sh_send, sh_recv, in_send, in_recv, fw_send, fw_recv,
):
    d = lax.axis_index("dp")
    q = lax.axis_index("mp")
    rows = ow.shape[0]
    ws = ow.shape[1] // heads
    tokens = act.shape[0]
    half = heads // 2
    sib = flip(q, 1)

    def remote(src, dst, send, arrive, where):
        return pltpu.make_async_remote_copy(
            src_ref=src, dst_ref=dst, send_sem=send, recv_sem=arrive,
            device_id=where, device_id_type=MESH,
        )

    def cols(s):
        return pl.ds(pl.multiple_of(lax.rem(q + s, heads) * ws, ws), ws)

    def fetch(s):
        return pltpu.make_async_copy(og.at[:, cols(s)], og_buf.at[s % 2], og_sem.at[s % 2])

    def reduce_copy(s, k):
        peer = flip(d, k)
        return remote(part.at[s, peer], recv.at[s, k - 1], rs_send.at[s, k - 1],
                      rs_recv.at[s, k - 1], {"dp": peer})

    def head_copy(s):
        return remote(w_buf.at[:, cols(s)], w_cols.at[q, d], a2a_send.at[s], a2a_recv.at[s],
                      {"mp": lax.rem(q + s, heads)})

    def gather_copy(s, k):
        block = w_cols.at[lax.rem(q - s + heads, heads), d]
        return remote(block, block, ag_send.at[s, k - 1], ag_recv.at[s, k - 1],
                      {"dp": flip(d, k)})

    def shift_copies(s):
        pairs = ((w_buf.at[:, cols(s)], nxt_w), (m_half.at[s], nxt_m), (v_half.at[s], nxt_v))
        return [
            remote(src, dst.at[:, cols(s)], sh_send.at[s, j], sh_recv.at[s, j], {"dp": d - 1})
            for j, (src, dst) in enumerate(pairs)
        ]

    def input_copy(j):
        return remote(nin, in_buf.at[q], in_send.at[j], in_recv.at[j],
                      {"mp": lax.rem(q + 2 * j, heads)})

    def sibling_copy(j):
        b = lax.rem(q - 2 * j + heads, heads)
        return remote(nin if j == 0 else in_buf.at[b], in_buf.at[b], fw_send.at[j],
                      fw_recv.at[j], {"mp": sib})

    olds = [
        pltpu.make_async_copy(src, dst, old_sem.at[j])
        for j, (src, dst) in enumerate(
            ((ow, ow_buf), (om, om_buf), (ov, ov_buf), (nin, in_buf.at[q]))
        )
    ]
    fetch(0).start()
    for copy in olds:
        copy.start()

    barrier = pltpu.get_barrier_semaphore()
    for k in range(1, owners):
        pl.semaphore_signal(barrier, inc=1, device_id={"dp": flip(d, k)}, device_id_type=MESH)
    for k in range(1, heads):
        pl.semaphore_signal(
            barrier, inc=1, device_id={"mp": lax.rem(q + k, heads)}, device_id_type=MESH
        )
    pl.semaphore_wait(barrier, owners + heads - 2)

    def grad_step(s, carry):
        @pl.when(s + 1 < heads)
        def _():
            fetch(s + 1).start()

        fetch(s).wait()
        g = lax.dot_general(
            act[...], og_buf[s % 2], (((0,), (0,)), ((), ())),
            preferred_element_type=jnp.float32,
        )
        for o in range(owners):
            piece = g[o * rows:(o + 1) * rows]
            part[s, o] = piece.astype(jnp.bfloat16)

            @pl.when(d == o)
            def _():
                own[s] = piece

        for k in range(1, owners):
            reduce_copy(s, k).start()
        return carry

    lax.fori_loop(0, heads, grad_step, 0)
    for j in range(1, half):
        input_copy(j).start()
    sibling_copy(0).start()
    acc[...] = jnp.zeros_like(acc)
    for copy in olds:
        copy.wait()

    def forward(s):
        @pl.when(s > 0)
        def _():
            head_copy(s).wait_recv()

        for k in range(1, owners):
            gather_copy(s, k).start()

    def adam_step(s, carry):
        c = cols(s)
        g = own[s]
        for k in range(1, owners):
            reduce_copy(s, k).wait_recv()
            g = g + recv[s, k - 1].astype(jnp.float32)
        m = 0.9 * om_buf[:, c] + 0.1 * g
        v = 0.95 * ov_buf[:, c] + 0.05 * g * g
        update = m * fix[0] / (jnp.sqrt(v * fix[1]) + 1e-08)
        w = (ow_buf[:, c].astype(jnp.float32) - 0.01 * update).astype(jnp.bfloat16)
        m_buf[:, c] = m
        v_buf[:, c] = v
        w_buf[:, c] = w
        m_half[s] = m.astype(jnp.bfloat16)
        v_half[s] = v.astype(jnp.bfloat16)

        @pl.when(s == 0)
        def _():
            w_cols[q, d] = w

        @pl.when(s > 0)
        def _():
            head_copy(s).start()
            forward(s - 1)

        @pl.when(d > 0)
        def _():
            for copy in shift_copies(s):
                copy.start()

        return carry

    lax.fori_loop(0, heads, adam_step, 0)
    forward(heads - 1)
    news = [
        pltpu.make_async_copy(src, dst, new_sem.at[j])
        for j, (src, dst) in enumerate(((w_buf, new_w), (m_buf, new_m), (v_buf, new_v)))
    ]
    for copy in news:
        copy.start()
    for j in range(1, half):
        input_copy(j).wait_recv()
        sibling_copy(j).start()
    for j in range(half):
        sibling_copy(j).wait_recv()

    tile = min(256, tokens)

    def output_step(s, carry):
        p = lax.rem(q - s + heads, heads)
        for k in range(1, owners):
            gather_copy(s, k).wait_recv()
        w = w_cols[p].reshape(owners * rows, ws)

        def rows_step(r, inner):
            at = pl.ds(pl.multiple_of(r * tile, tile), tile)
            acc[at, :] += jnp.dot(in_buf[p, at, :], w, preferred_element_type=jnp.float32)
            return inner

        return lax.fori_loop(0, tokens // tile, rows_step, carry)

    lax.fori_loop(0, heads, output_step, 0)
    out[...] = acc[...].astype(jnp.bfloat16)

    for copy in news:
        copy.wait()
    for j in range(1, half):
        input_copy(j).wait_send()
    for j in range(half):
        sibling_copy(j).wait_send()

    def drain(s, carry):
        for k in range(1, owners):
            reduce_copy(s, k).wait_send()
            gather_copy(s, k).wait_send()

        @pl.when(s > 0)
        def _():
            head_copy(s).wait_send()

        @pl.when(d > 0)
        def _():
            for copy in shift_copies(s):
                copy.wait_send()

        @pl.when(d < owners - 1)
        def _():
            for copy in shift_copies(s):
                copy.wait_recv()

        return carry

    lax.fori_loop(0, heads, drain, 0)


def body(activations, out_grad, old_weight, old_first, old_second, step, next_input):
    owners = lax.axis_size("dp")
    heads = lax.axis_size("mp")
    owner = lax.axis_index("dp")
    _, rows, width = old_weight.shape
    tokens, part_rows = activations.shape
    held_rows = rows * owners
    shard_rows = (held_rows + owners - 2) // (owners - 1)
    ws = width // heads
    step_float = step[0].astype(jnp.float32)
    first_fix = 1.0 - jnp.power(jnp.float32(0.9), step_float)
    second_fix = 1.0 - jnp.power(jnp.float32(0.95), step_float)
    fix = jnp.stack([1.0 / first_fix, 1.0 / second_fix])

    bf16, f32 = jnp.bfloat16, jnp.float32
    full = jax.ShapeDtypeStruct((rows, width), bf16)
    wide = jax.ShapeDtypeStruct((rows, width), f32)
    anywhere = pl.BlockSpec(memory_space=pl.ANY)
    vmem = pl.BlockSpec(memory_space=pltpu.VMEM)
    dma = pltpu.SemaphoreType.DMA
    half = heads // 2
    new_w, nxt_w, new_m, nxt_m, new_v, nxt_v, output = pl.pallas_call(
        functools.partial(kernel, owners, heads),
        out_shape=(full, full, wide, full, wide, full, jax.ShapeDtypeStruct((tokens, ws), bf16)),
        in_specs=[pl.BlockSpec(memory_space=pltpu.SMEM), vmem] + [anywhere] * 5,
        out_specs=(anywhere,) * 6 + (vmem,),
        scratch_shapes=[
            pltpu.VMEM((2, tokens, ws), bf16),
            pltpu.VMEM((heads, owners, rows, ws), bf16),
            pltpu.VMEM((heads, rows, ws), f32),
            pltpu.VMEM((heads, owners - 1, rows, ws), bf16),
            pltpu.VMEM((rows, width), bf16),
            pltpu.VMEM((rows, width), f32),
            pltpu.VMEM((rows, width), f32),
            pltpu.VMEM((rows, width), bf16),
            pltpu.VMEM((rows, width), f32),
            pltpu.VMEM((rows, width), f32),
            pltpu.VMEM((heads, rows, ws), bf16),
            pltpu.VMEM((heads, rows, ws), bf16),
            pltpu.VMEM((heads, owners, rows, ws), bf16),
            pltpu.VMEM((heads, tokens, part_rows), bf16),
            pltpu.VMEM((tokens, ws), f32),
            dma((2,)), dma((4,)), dma((3,)),
            dma((heads, owners - 1)), dma((heads, owners - 1)),
            dma((heads,)), dma((heads,)),
            dma((heads, owners - 1)), dma((heads, owners - 1)),
            dma((heads, 3)), dma((heads, 3)),
            dma((half,)), dma((half,)), dma((half,)), dma((half,)),
        ],
        compiler_params=pltpu.CompilerParams(
            collective_id=0, has_side_effects=True, vmem_limit_bytes=56 * MIB
        ),
    )(fix, activations, out_grad, old_weight[0], old_first[0], old_second[0], next_input)

    begin = owner * (shard_rows - rows)

    def mine(block, behind):
        behind = jnp.where(owner == owners - 1, 0, behind.astype(block.dtype))
        both = jnp.concatenate([block, behind, jnp.zeros((shard_rows, width), block.dtype)], 0)
        return lax.dynamic_slice_in_dim(both, begin, shard_rows, 0)[None]

    return (mine(new_w, nxt_w), mine(new_m, nxt_m), mine(new_v, nxt_v), output)


def solution(mesh):
    return jax.shard_map(
        body,
        mesh=mesh,
        in_specs=(
            P("dp", "mp"),
            P("dp", None),
            P("mp", "dp", None),
            P("mp", "dp", None),
            P("mp", "dp", None),
            P(),
            P("dp", "mp"),
        ),
        out_specs=(P("mp", "dp", None), P("mp", "dp", None), P("mp", "dp", None), P("dp", "mp")),
        check_vma=False,
    )
```

```python
import functools

import jax
import jax.numpy as jnp
from jax import lax
from jax.experimental import pallas as pl
from jax.experimental.pallas import tpu as pltpu
from jax.sharding import PartitionSpec as P

MESH = pl.DeviceIdType.MESH
MIB = 1 << 20


def flip(i, k):
    for bit in (1, 2, 4, 8, 16):
        if k & bit:
            i = i + bit * (1 - 2 * ((i // bit) % 2))
    return i


def kernel(
    owners, heads,
    fix, act, og, ow, om, ov, nin,
    new_w, nxt_w, new_m, nxt_m, new_v, nxt_v, out,
    og_buf, part, own, recv, ow_buf, om_buf, ov_buf, w_buf, m_buf, v_buf, m_half, v_half,
    w_cols, in_buf, acc,
    og_sem, old_sem, new_sem, rs_send, rs_recv, a2a_send, a2a_recv, ag_send, ag_recv,
    sh_send, sh_recv, back_send, back_recv, in_send, in_recv, fw_send, fw_recv,
):
    d = lax.axis_index("dp")
    q = lax.axis_index("mp")
    rows = ow.shape[0]
    ws = ow.shape[1] // heads
    tokens = act.shape[0]
    half = heads // 2
    sib = flip(q, 1)

    def remote(src, dst, send, arrive, where):
        return pltpu.make_async_remote_copy(
            src_ref=src, dst_ref=dst, send_sem=send, recv_sem=arrive,
            device_id=where, device_id_type=MESH,
        )

    def cols(s):
        return pl.ds(pl.multiple_of(lax.rem(q + s, heads) * ws, ws), ws)

    def fetch(s):
        return pltpu.make_async_copy(og.at[:, cols(s)], og_buf.at[s % 2], og_sem.at[s % 2])

    def reduce_copy(s, k):
        peer = flip(d, k)
        return remote(part.at[s, peer], recv.at[s, k - 1], rs_send.at[s, k - 1],
                      rs_recv.at[s, k - 1], {"dp": peer})

    def head_copy(s):
        return remote(w_buf.at[:, cols(s)], w_cols.at[q, d], a2a_send.at[s], a2a_recv.at[s],
                      {"mp": lax.rem(q + s, heads)})

    def gather_copy(s, k):
        block = w_cols.at[lax.rem(q - s + heads, heads), d]
        return remote(block, block, ag_send.at[s, k - 1], ag_recv.at[s, k - 1],
                      {"dp": flip(d, k)})

    def shift_copies(s):
        pairs = ((m_half.at[s], nxt_m), (v_half.at[s], nxt_v))
        return [
            remote(src, dst.at[:, cols(s)], sh_send.at[s, j], sh_recv.at[s, j], {"dp": d - 1})
            for j, (src, dst) in enumerate(pairs)
        ]

    behind = lax.rem(d + 1, owners)

    def back_own():
        return pltpu.make_async_copy(
            w_cols.at[q, behind], nxt_w.at[:, cols(0)], back_send.at[0]
        )

    def back_copy(s):
        p = lax.rem(q - s + heads, heads)
        return remote(w_cols.at[p, behind], nxt_w.at[:, cols(0)], back_send.at[s],
                      back_recv.at[s], {"mp": p})

    def input_copy(j):
        return remote(nin, in_buf.at[q], in_send.at[j], in_recv.at[j],
                      {"mp": lax.rem(q + 2 * j, heads)})

    def sibling_copy(j):
        b = lax.rem(q - 2 * j + heads, heads)
        return remote(nin if j == 0 else in_buf.at[b], in_buf.at[b], fw_send.at[j],
                      fw_recv.at[j], {"mp": sib})

    olds = [
        pltpu.make_async_copy(src, dst, old_sem.at[j])
        for j, (src, dst) in enumerate(
            ((ow, ow_buf), (om, om_buf), (ov, ov_buf), (nin, in_buf.at[q]))
        )
    ]
    fetch(0).start()
    for copy in olds:
        copy.start()

    barrier = pltpu.get_barrier_semaphore()
    for k in range(1, owners):
        pl.semaphore_signal(barrier, inc=1, device_id={"dp": flip(d, k)}, device_id_type=MESH)
    for k in range(1, heads):
        pl.semaphore_signal(
            barrier, inc=1, device_id={"mp": lax.rem(q + k, heads)}, device_id_type=MESH
        )
    pl.semaphore_wait(barrier, owners + heads - 2)

    def grad_step(s, carry):
        @pl.when(s + 1 < heads)
        def _():
            fetch(s + 1).start()

        fetch(s).wait()
        g = lax.dot_general(
            act[...], og_buf[s % 2], (((0,), (0,)), ((), ())),
            preferred_element_type=jnp.float32,
        )
        for o in range(owners):
            piece = g[o * rows:(o + 1) * rows]
            part[s, o] = piece.astype(jnp.bfloat16)

            @pl.when(d == o)
            def _():
                own[s] = piece

        for k in range(1, owners):
            reduce_copy(s, k).start()
        return carry

    lax.fori_loop(0, heads, grad_step, 0)
    for j in range(1, half):
        input_copy(j).start()
    sibling_copy(0).start()
    acc[...] = jnp.zeros_like(acc)
    for copy in olds:
        copy.wait()

    def forward(s):
        @pl.when(s > 0)
        def _():
            head_copy(s).wait_recv()

        for k in range(1, owners):
            gather_copy(s, k).start()

    def adam_step(s, carry):
        c = cols(s)
        g = own[s]
        for k in range(1, owners):
            reduce_copy(s, k).wait_recv()
            g = g + recv[s, k - 1].astype(jnp.float32)
        m = 0.9 * om_buf[:, c] + 0.1 * g
        v = 0.95 * ov_buf[:, c] + 0.05 * g * g
        update = m * fix[0] / (jnp.sqrt(v * fix[1]) + 1e-08)
        w = (ow_buf[:, c].astype(jnp.float32) - 0.01 * update).astype(jnp.bfloat16)
        m_buf[:, c] = m
        v_buf[:, c] = v
        w_buf[:, c] = w
        m_half[s] = m.astype(jnp.bfloat16)
        v_half[s] = v.astype(jnp.bfloat16)

        @pl.when(s == 0)
        def _():
            w_cols[q, d] = w

        @pl.when(s > 0)
        def _():
            head_copy(s).start()
            forward(s - 1)

        @pl.when(d > 0)
        def _():
            for copy in shift_copies(s):
                copy.start()

        return carry

    lax.fori_loop(0, heads, adam_step, 0)
    forward(heads - 1)
    news = [
        pltpu.make_async_copy(src, dst, new_sem.at[j])
        for j, (src, dst) in enumerate(((w_buf, new_w), (m_buf, new_m), (v_buf, new_v)))
    ]
    for copy in news:
        copy.start()
    for j in range(1, half):
        input_copy(j).wait_recv()
        sibling_copy(j).start()
    for j in range(half):
        sibling_copy(j).wait_recv()

    tile = min(256, tokens)

    def output_step(s, carry):
        p = lax.rem(q - s + heads, heads)
        for k in range(1, owners):
            gather_copy(s, k).wait_recv()

        @pl.when(jnp.logical_and(d < owners - 1, s == 0))
        def _():
            back_own().start()

        @pl.when(jnp.logical_and(d < owners - 1, s > 0))
        def _():
            back_copy(s).start()

        w = w_cols[p].reshape(owners * rows, ws)

        def rows_step(r, inner):
            at = pl.ds(pl.multiple_of(r * tile, tile), tile)
            acc[at, :] += jnp.dot(in_buf[p, at, :], w, preferred_element_type=jnp.float32)
            return inner

        return lax.fori_loop(0, tokens // tile, rows_step, carry)

    lax.fori_loop(0, heads, output_step, 0)
    out[...] = acc[...].astype(jnp.bfloat16)

    for copy in news:
        copy.wait()
    for j in range(1, half):
        input_copy(j).wait_send()
    for j in range(half):
        sibling_copy(j).wait_send()

    def drain(s, carry):
        for k in range(1, owners):
            reduce_copy(s, k).wait_send()
            gather_copy(s, k).wait_send()

        @pl.when(s > 0)
        def _():
            head_copy(s).wait_send()

        @pl.when(d > 0)
        def _():
            for copy in shift_copies(s):
                copy.wait_send()

        @pl.when(d < owners - 1)
        def _():
            for copy in shift_copies(s):
                copy.wait_recv()

            @pl.when(s == 0)
            def _():
                back_own().wait()

            @pl.when(s > 0)
            def _():
                back_copy(s).wait_send()
                remote(w_cols.at[q, behind], nxt_w.at[:, cols(s)], back_send.at[s],
                       back_recv.at[s], {"mp": lax.rem(q + s, heads)}).wait_recv()

        return carry

    lax.fori_loop(0, heads, drain, 0)


def body(activations, out_grad, old_weight, old_first, old_second, step, next_input):
    owners = lax.axis_size("dp")
    heads = lax.axis_size("mp")
    owner = lax.axis_index("dp")
    _, rows, width = old_weight.shape
    tokens, part_rows = activations.shape
    held_rows = rows * owners
    shard_rows = (held_rows + owners - 2) // (owners - 1)
    ws = width // heads
    step_float = step[0].astype(jnp.float32)
    first_fix = 1.0 - jnp.power(jnp.float32(0.9), step_float)
    second_fix = 1.0 - jnp.power(jnp.float32(0.95), step_float)
    fix = jnp.stack([1.0 / first_fix, 1.0 / second_fix])

    bf16, f32 = jnp.bfloat16, jnp.float32
    full = jax.ShapeDtypeStruct((rows, width), bf16)
    wide = jax.ShapeDtypeStruct((rows, width), f32)
    anywhere = pl.BlockSpec(memory_space=pl.ANY)
    vmem = pl.BlockSpec(memory_space=pltpu.VMEM)
    dma = pltpu.SemaphoreType.DMA
    half = heads // 2
    new_w, nxt_w, new_m, nxt_m, new_v, nxt_v, output = pl.pallas_call(
        functools.partial(kernel, owners, heads),
        out_shape=(full, full, wide, full, wide, full, jax.ShapeDtypeStruct((tokens, ws), bf16)),
        in_specs=[pl.BlockSpec(memory_space=pltpu.SMEM), vmem] + [anywhere] * 5,
        out_specs=(anywhere,) * 6 + (vmem,),
        scratch_shapes=[
            pltpu.VMEM((2, tokens, ws), bf16),
            pltpu.VMEM((heads, owners, rows, ws), bf16),
            pltpu.VMEM((heads, rows, ws), f32),
            pltpu.VMEM((heads, owners - 1, rows, ws), bf16),
            pltpu.VMEM((rows, width), bf16),
            pltpu.VMEM((rows, width), f32),
            pltpu.VMEM((rows, width), f32),
            pltpu.VMEM((rows, width), bf16),
            pltpu.VMEM((rows, width), f32),
            pltpu.VMEM((rows, width), f32),
            pltpu.VMEM((heads, rows, ws), bf16),
            pltpu.VMEM((heads, rows, ws), bf16),
            pltpu.VMEM((heads, owners, rows, ws), bf16),
            pltpu.VMEM((heads, tokens, part_rows), bf16),
            pltpu.VMEM((tokens, ws), f32),
            dma((2,)), dma((4,)), dma((3,)),
            dma((heads, owners - 1)), dma((heads, owners - 1)),
            dma((heads,)), dma((heads,)),
            dma((heads, owners - 1)), dma((heads, owners - 1)),
            dma((heads, 2)), dma((heads, 2)), dma((heads,)), dma((heads,)),
            dma((half,)), dma((half,)), dma((half,)), dma((half,)),
        ],
        compiler_params=pltpu.CompilerParams(
            collective_id=0, has_side_effects=True, vmem_limit_bytes=56 * MIB
        ),
    )(fix, activations, out_grad, old_weight[0], old_first[0], old_second[0], next_input)

    begin = owner * (shard_rows - rows)

    def mine(block, behind):
        behind = jnp.where(owner == owners - 1, 0, behind.astype(block.dtype))
        both = jnp.concatenate([block, behind, jnp.zeros((shard_rows, width), block.dtype)], 0)
        return lax.dynamic_slice_in_dim(both, begin, shard_rows, 0)[None]

    return (mine(new_w, nxt_w), mine(new_m, nxt_m), mine(new_v, nxt_v), output)


def solution(mesh):
    return jax.shard_map(
        body,
        mesh=mesh,
        in_specs=(
            P("dp", "mp"),
            P("dp", None),
            P("mp", "dp", None),
            P("mp", "dp", None),
            P("mp", "dp", None),
            P(),
            P("dp", "mp"),
        ),
        out_specs=(P("mp", "dp", None), P("mp", "dp", None), P("mp", "dp", None), P("dp", "mp")),
        check_vma=False,
    )
```

```python
import functools

import jax
import jax.numpy as jnp
from jax import lax
from jax.experimental import pallas as pl
from jax.experimental.pallas import tpu as pltpu
from jax.sharding import PartitionSpec as P

MESH = pl.DeviceIdType.MESH
MIB = 1 << 20


def flip(i, k):
    for bit in (1, 2, 4, 8, 16):
        if k & bit:
            i = i + bit * (1 - 2 * ((i // bit) % 2))
    return i


def kernel(
    owners, heads,
    fix, act, og, ow, om, ov, nin,
    new_w, nxt_w, new_m, nxt_m, new_v, nxt_v, out,
    og_buf, part, own, recv, ow_buf, om_buf, ov_buf, w_buf, m_buf, v_buf, m_half, v_half,
    w_cols, in_buf, acc,
    og_sem, old_sem, new_sem, rs_send, rs_recv, a2a_send, a2a_recv, ag_send, ag_recv,
    sh_send, sh_recv, back_send, back_recv, in_send, in_recv, fw_send, fw_recv,
):
    d = lax.axis_index("dp")
    q = lax.axis_index("mp")
    rows = ow.shape[0]
    ws = ow.shape[1] // heads
    tokens = act.shape[0]
    half = heads // 2
    sib = flip(q, 1)

    def remote(src, dst, send, arrive, where):
        return pltpu.make_async_remote_copy(
            src_ref=src, dst_ref=dst, send_sem=send, recv_sem=arrive,
            device_id=where, device_id_type=MESH,
        )

    def cols(s):
        return pl.ds(pl.multiple_of(lax.rem(q + s, heads) * ws, ws), ws)

    def fetch(s):
        return pltpu.make_async_copy(og.at[:, cols(s)], og_buf.at[s % 2], og_sem.at[s % 2])

    def reduce_copy(s, k):
        peer = flip(d, k)
        return remote(part.at[s, peer], recv.at[s, k - 1], rs_send.at[s, k - 1],
                      rs_recv.at[s, k - 1], {"dp": peer})

    def head_copy(s):
        return remote(w_buf.at[:, cols(s)], w_cols.at[q, d], a2a_send.at[s], a2a_recv.at[s],
                      {"mp": lax.rem(q + s, heads)})

    def gather_copy(s, k):
        block = w_cols.at[lax.rem(q - s + heads, heads), d]
        return remote(block, block, ag_send.at[s, k - 1], ag_recv.at[s, k - 1],
                      {"dp": flip(d, k)})

    def shift_copies(s, sender):
        short = -(-rows // (owners - 1))
        n = min(rows, -(-short * sender // 16) * 16)
        top = pl.ds(0, n)
        pairs = ((m_half.at[s, top], nxt_m), (v_half.at[s, top], nxt_v))
        return [
            remote(src, dst.at[top, cols(s)], sh_send.at[s, j], sh_recv.at[s, j], {"dp": d - 1})
            for j, (src, dst) in enumerate(pairs)
        ]

    behind = lax.rem(d + 1, owners)

    def back_own():
        return pltpu.make_async_copy(
            w_cols.at[q, behind], nxt_w.at[:, cols(0)], back_send.at[0]
        )

    def back_copy(s):
        p = lax.rem(q - s + heads, heads)
        return remote(w_cols.at[p, behind], nxt_w.at[:, cols(0)], back_send.at[s],
                      back_recv.at[s], {"mp": p})

    def input_copy(j):
        return remote(nin, in_buf.at[q], in_send.at[j], in_recv.at[j],
                      {"mp": lax.rem(q + 2 * j, heads)})

    def sibling_copy(j):
        b = lax.rem(q - 2 * j + heads, heads)
        return remote(nin if j == 0 else in_buf.at[b], in_buf.at[b], fw_send.at[j],
                      fw_recv.at[j], {"mp": sib})

    olds = [
        pltpu.make_async_copy(src, dst, old_sem.at[j])
        for j, (src, dst) in enumerate(
            ((ow, ow_buf), (om, om_buf), (ov, ov_buf), (nin, in_buf.at[q]))
        )
    ]
    fetch(0).start()
    for copy in olds:
        copy.start()

    barrier = pltpu.get_barrier_semaphore()
    for k in range(1, owners):
        pl.semaphore_signal(barrier, inc=1, device_id={"dp": flip(d, k)}, device_id_type=MESH)
    for k in range(1, heads):
        pl.semaphore_signal(
            barrier, inc=1, device_id={"mp": lax.rem(q + k, heads)}, device_id_type=MESH
        )
    pl.semaphore_wait(barrier, owners + heads - 2)

    def grad_step(s, carry):
        @pl.when(s + 1 < heads)
        def _():
            fetch(s + 1).start()

        fetch(s).wait()
        g = lax.dot_general(
            act[...], og_buf[s % 2], (((0,), (0,)), ((), ())),
            preferred_element_type=jnp.float32,
        )
        for o in range(owners):
            piece = g[o * rows:(o + 1) * rows]
            part[s, o] = piece.astype(jnp.bfloat16)

            @pl.when(d == o)
            def _():
                own[s] = piece

        for k in range(1, owners):
            reduce_copy(s, k).start()
        return carry

    lax.fori_loop(0, heads, grad_step, 0)
    for j in range(1, half):
        input_copy(j).start()
    sibling_copy(0).start()
    acc[...] = jnp.zeros_like(acc)
    for copy in olds:
        copy.wait()

    def forward(s):
        @pl.when(s > 0)
        def _():
            head_copy(s).wait_recv()

        for k in range(1, owners):
            gather_copy(s, k).start()

    def adam_step(s, carry):
        c = cols(s)
        g = own[s]
        for k in range(1, owners):
            reduce_copy(s, k).wait_recv()
            g = g + recv[s, k - 1].astype(jnp.float32)
        m = 0.9 * om_buf[:, c] + 0.1 * g
        v = 0.95 * ov_buf[:, c] + 0.05 * g * g
        update = m * fix[0] / (jnp.sqrt(v * fix[1]) + 1e-08)
        w = (ow_buf[:, c].astype(jnp.float32) - 0.01 * update).astype(jnp.bfloat16)
        m_buf[:, c] = m
        v_buf[:, c] = v
        w_buf[:, c] = w
        m_half[s] = m.astype(jnp.bfloat16)
        v_half[s] = v.astype(jnp.bfloat16)

        @pl.when(s == 0)
        def _():
            w_cols[q, d] = w

        @pl.when(s > 0)
        def _():
            head_copy(s).start()
            forward(s - 1)

        for sender in range(1, owners):
            @pl.when(d == sender)
            def _():
                for copy in shift_copies(s, sender):
                    copy.start()

        return carry

    lax.fori_loop(0, heads, adam_step, 0)
    forward(heads - 1)
    news = [
        pltpu.make_async_copy(src, dst, new_sem.at[j])
        for j, (src, dst) in enumerate(((w_buf, new_w), (m_buf, new_m), (v_buf, new_v)))
    ]
    for copy in news:
        copy.start()
    for j in range(1, half):
        input_copy(j).wait_recv()
        sibling_copy(j).start()
    for j in range(half):
        sibling_copy(j).wait_recv()

    tile = min(256, tokens)

    def output_step(s, carry):
        p = lax.rem(q - s + heads, heads)
        for k in range(1, owners):
            gather_copy(s, k).wait_recv()

        @pl.when(jnp.logical_and(d < owners - 1, s == 0))
        def _():
            back_own().start()

        @pl.when(jnp.logical_and(d < owners - 1, s > 0))
        def _():
            back_copy(s).start()

        w = w_cols[p].reshape(owners * rows, ws)

        def rows_step(r, inner):
            at = pl.ds(pl.multiple_of(r * tile, tile), tile)
            acc[at, :] += jnp.dot(in_buf[p, at, :], w, preferred_element_type=jnp.float32)
            return inner

        return lax.fori_loop(0, tokens // tile, rows_step, carry)

    lax.fori_loop(0, heads, output_step, 0)
    out[...] = acc[...].astype(jnp.bfloat16)

    for copy in news:
        copy.wait()
    for j in range(1, half):
        input_copy(j).wait_send()
    for j in range(half):
        sibling_copy(j).wait_send()

    def drain(s, carry):
        for k in range(1, owners):
            reduce_copy(s, k).wait_send()
            gather_copy(s, k).wait_send()

        @pl.when(s > 0)
        def _():
            head_copy(s).wait_send()

        for sender in range(1, owners):
            @pl.when(d == sender)
            def _():
                for copy in shift_copies(s, sender):
                    copy.wait_send()

            @pl.when(d == sender - 1)
            def _():
                for copy in shift_copies(s, sender):
                    copy.wait_recv()

        @pl.when(d < owners - 1)
        def _():
            @pl.when(s == 0)
            def _():
                back_own().wait()

            @pl.when(s > 0)
            def _():
                back_copy(s).wait_send()
                remote(w_cols.at[q, behind], nxt_w.at[:, cols(s)], back_send.at[s],
                       back_recv.at[s], {"mp": lax.rem(q + s, heads)}).wait_recv()

        return carry

    lax.fori_loop(0, heads, drain, 0)


def body(activations, out_grad, old_weight, old_first, old_second, step, next_input):
    owners = lax.axis_size("dp")
    heads = lax.axis_size("mp")
    owner = lax.axis_index("dp")
    _, rows, width = old_weight.shape
    tokens, part_rows = activations.shape
    held_rows = rows * owners
    shard_rows = (held_rows + owners - 2) // (owners - 1)
    ws = width // heads
    step_float = step[0].astype(jnp.float32)
    first_fix = 1.0 - jnp.power(jnp.float32(0.9), step_float)
    second_fix = 1.0 - jnp.power(jnp.float32(0.95), step_float)
    fix = jnp.stack([1.0 / first_fix, 1.0 / second_fix])

    bf16, f32 = jnp.bfloat16, jnp.float32
    full = jax.ShapeDtypeStruct((rows, width), bf16)
    wide = jax.ShapeDtypeStruct((rows, width), f32)
    anywhere = pl.BlockSpec(memory_space=pl.ANY)
    vmem = pl.BlockSpec(memory_space=pltpu.VMEM)
    dma = pltpu.SemaphoreType.DMA
    half = heads // 2
    new_w, nxt_w, new_m, nxt_m, new_v, nxt_v, output = pl.pallas_call(
        functools.partial(kernel, owners, heads),
        out_shape=(full, full, wide, full, wide, full, jax.ShapeDtypeStruct((tokens, ws), bf16)),
        in_specs=[pl.BlockSpec(memory_space=pltpu.SMEM), vmem] + [anywhere] * 5,
        out_specs=(anywhere,) * 6 + (vmem,),
        scratch_shapes=[
            pltpu.VMEM((2, tokens, ws), bf16),
            pltpu.VMEM((heads, owners, rows, ws), bf16),
            pltpu.VMEM((heads, rows, ws), f32),
            pltpu.VMEM((heads, owners - 1, rows, ws), bf16),
            pltpu.VMEM((rows, width), bf16),
            pltpu.VMEM((rows, width), f32),
            pltpu.VMEM((rows, width), f32),
            pltpu.VMEM((rows, width), bf16),
            pltpu.VMEM((rows, width), f32),
            pltpu.VMEM((rows, width), f32),
            pltpu.VMEM((heads, rows, ws), bf16),
            pltpu.VMEM((heads, rows, ws), bf16),
            pltpu.VMEM((heads, owners, rows, ws), bf16),
            pltpu.VMEM((heads, tokens, part_rows), bf16),
            pltpu.VMEM((tokens, ws), f32),
            dma((2,)), dma((4,)), dma((3,)),
            dma((heads, owners - 1)), dma((heads, owners - 1)),
            dma((heads,)), dma((heads,)),
            dma((heads, owners - 1)), dma((heads, owners - 1)),
            dma((heads, 2)), dma((heads, 2)), dma((heads,)), dma((heads,)),
            dma((half,)), dma((half,)), dma((half,)), dma((half,)),
        ],
        compiler_params=pltpu.CompilerParams(
            collective_id=0, has_side_effects=True, vmem_limit_bytes=56 * MIB
        ),
    )(fix, activations, out_grad, old_weight[0], old_first[0], old_second[0], next_input)

    begin = owner * (shard_rows - rows)

    def mine(block, behind):
        behind = jnp.where(owner == owners - 1, 0, behind.astype(block.dtype))
        both = jnp.concatenate([block, behind, jnp.zeros((shard_rows, width), block.dtype)], 0)
        return lax.dynamic_slice_in_dim(both, begin, shard_rows, 0)[None]

    return (mine(new_w, nxt_w), mine(new_m, nxt_m), mine(new_v, nxt_v), output)


def solution(mesh):
    return jax.shard_map(
        body,
        mesh=mesh,
        in_specs=(
            P("dp", "mp"),
            P("dp", None),
            P("mp", "dp", None),
            P("mp", "dp", None),
            P("mp", "dp", None),
            P(),
            P("dp", "mp"),
        ),
        out_specs=(P("mp", "dp", None), P("mp", "dp", None), P("mp", "dp", None), P("dp", "mp")),
        check_vma=False,
    )
```
